512 devices in a mesh: grp: 4 (over x_lo, core), resp: 16 (over x_hi, z), tp: 8 (over y).
Axes of the slice: x: 4 (x_hi: 2, x_lo: 2; x = x_hi * 2 + x_lo), y: 8, z: 8, core: 2. Of those that a mesh axis runs over, the one named last changes fastest.
Arguments:
- queries: bfloat16 [16384, 8192], P(('grp', 'resp'), 'tp'), parts along dimension 0, may hold values from -6 to 6
- own_keys: bfloat16 [16384, 1024], P(('grp', 'resp'), 'tp'), parts along dimension 0, may hold values from -5 to 5
- own_values: bfloat16 [16384, 1024], P(('grp', 'resp'), 'tp'), parts along dimension 0, may hold values from -5 to 5
- prefix_keys: bfloat16 [8192, 1024], P(('grp', 'resp'), 'tp'), parts along dimension 0, may hold values from -6 to 6
- prefix_values: bfloat16 [8192, 1024], P(('grp', 'resp'), 'tp'), parts along dimension 0, may hold values from -5 to 5
- out_grad: bfloat16 [16384, 8192], P(('grp', 'resp'), 'tp'), parts along dimension 0, may hold values from -6 to 6
- lengths: int32 [64], P(('grp', 'resp')), parts along dimension 0, may hold values from 32 to 256, as said below
- advantage_sign: int32 [64], P(('grp', 'resp')), parts along dimension 0, may hold values from 0 to 1
Outputs:
- query_grad: bfloat16 [16384, 8192], P(('grp', 'resp'), 'tp'), parts along dimension 0
- own_key_grad: bfloat16 [16384, 1024], P(('grp', 'resp'), 'tp'), parts along dimension 0
- own_value_grad: bfloat16 [16384, 1024], P(('grp', 'resp'), 'tp'), parts along dimension 0
- prefix_key_grad: bfloat16 [8192, 1024], P(('grp', 'resp'), 'tp'), parts along dimension 0
- prefix_value_grad: bfloat16 [8192, 1024], P(('grp', 'resp'), 'tp'), parts along dimension 0
The draws below stay inside these ranges and needn't reach their ends.
There are 4 independent parts, one for each index of `grp`. The reference program is written for one: setup_inputs(seed, part) draws one part's arguments, and reference() takes and returns one part's arrays. A program takes and returns all parts, laid end to end along the dimension named above; each array names one. Nothing has to cross between parts.
Inputs may be any that keep to these rules, and one draw needn't show every extreme that they name: `lengths`: live tokens of each response; some response has exactly 256.
All inputs are finite; a program needn't handle non-finite values.
Results may differ from the reference program's by a relative error of at most 0.022.
Values may be sent and summed in bfloat16 or wider, within the bound.
A program may use at most 64 MiB of HBM per device.

```python
import math
import jax
import jax.numpy as jnp
from jax import lax

QH = 64
KVH = 8
DH = 128
RLEN = 256
RESPONSES = 16
PREFIX = 2048


def draw_queries(key, part):
    key = jax.random.fold_in(key, 1)
    shape = (RESPONSES * RLEN, QH * DH)
    values = jnp.clip(jax.random.normal(key, shape, jnp.float32), -4.0, 4.0)
    return values.astype(jnp.bfloat16)


def draw_prefix_keys(key, part):
    key = jax.random.fold_in(key, 2)
    shape = (PREFIX, KVH * DH)
    values = jnp.clip(jax.random.normal(key, shape, jnp.float32), -4.0, 4.0)
    return values.astype(jnp.bfloat16)


def draw_lengths(key, part):
    key = jax.random.fold_in(key, 3)
    index = jnp.arange(RESPONSES, dtype=jnp.int32)
    lowest = RLEN // 4 + 3 * RLEN // 4 * index // max(RESPONSES - 1, 1)
    jitter = jax.random.randint(jax.random.fold_in(key, 5), (RESPONSES,), -(RLEN // 8), RLEN // 8 + 1)
    values = jnp.clip(lowest + jitter, RLEN // 8, RLEN)
    longest = jax.random.randint(jax.random.fold_in(key, 7), (), RESPONSES // 2, RESPONSES)
    values = jnp.where(index == longest, RLEN, values)
    return values.astype(jnp.int32)


def set_ends(drawn, stream_key, least, largest):
    longest = drawn.shape.index(max(drawn.shape))
    spots = []
    for shift in (0, 1):
        where = [jax.random.randint(jax.random.fold_in(stream_key, axis), (), 0, length) for axis, length in enumerate(drawn.shape)]
        where[longest] = (where[longest] + shift) % drawn.shape[longest]
        spots.append(tuple(where))
    return drawn.at[spots[0]].set(least).at[spots[1]].set(largest)


def level_of(rng, extent, pieces, low, high):
    gain, own = 1.0, jax.random.fold_in(rng, 6)
    for dim, shards_of in pieces:
        steps = jnp.exp(jax.random.uniform(jax.random.fold_in(own, dim), (shards_of,), jnp.float32, low / len(pieces), high / len(pieces)))
        gain = gain * jnp.repeat(steps, extent[dim] // shards_of).reshape([-1 if axis == dim else 1 for axis in range(len(extent))])
    return gain


def gaussian(own_key, extent, deviation, bound, cuts=(), held_as=jnp.bfloat16):
    array = jax.random.normal(own_key, extent, jnp.float32) * deviation
    if len(cuts) > 0:
        array = level_of(own_key, extent, cuts, -0.22, 0.18) * array
    return jnp.clip(array, min=-bound, max=bound).astype(held_as)


def setup_inputs(seed: int = 0, part: int = 0) -> dict:
    streams_of = jax.random.split(jax.random.key(seed), 9)
    part_keys = jax.random.split(jax.random.fold_in(streams_of[8], part), 9)
    return {
        "queries": draw_queries(jax.random.fold_in(jax.random.fold_in(streams_of[8], part), 71), part),
        "own_keys": gaussian(part_keys[1], (RESPONSES * RLEN, KVH * DH), 1.0, 5.0, ((0, 16), (1, 8))),
        "own_values": gaussian(part_keys[2], (RESPONSES * RLEN, KVH * DH), 1.0, 5.0, ((0, 16), (1, 8))),
        "prefix_keys": draw_prefix_keys(jax.random.fold_in(jax.random.fold_in(streams_of[8], part), 71), part),
        "prefix_values": gaussian(part_keys[4], (PREFIX, KVH * DH), 1.0, 5.0, ((0, 16), (1, 8))),
        "out_grad": gaussian(part_keys[5], (RESPONSES * RLEN, QH * DH), 1.0, 6.0, ((0, 16), (1, 8))),
        "lengths": draw_lengths(jax.random.fold_in(jax.random.fold_in(streams_of[8], part), 71), part),
        "advantage_sign": set_ends(jax.random.randint(part_keys[7], (RESPONSES,), 0, 2), jax.random.fold_in(part_keys[7], 1), 0, 1).astype(jnp.int32),
    }


def product(form, left, right):
    return jnp.einsum(form, left.astype(jnp.float32), right.astype(jnp.float32), precision=lax.Precision.HIGHEST)

def attend(q_heads, g_heads, all_keys, all_values, visible, scale_factor):
    scores = jnp.where(visible, product('hgqd,khd->hgqk', q_heads, all_keys) * scale_factor, -jnp.inf)
    row_top = lax.optimization_barrier(jnp.max(scores, -1, keepdims=True))
    expo = jnp.exp(scores - row_top)
    prob_f = expo / lax.optimization_barrier(jnp.sum(expo, -1, keepdims=True))
    prob = prob_f.astype(jnp.bfloat16)
    attn = product('hgqk,khd->hgqd', prob, all_values)
    delta = lax.optimization_barrier(jnp.sum(g_heads.astype(jnp.float32) * attn, -1, keepdims=True))
    dprob = product('hgqd,khd->hgqk', g_heads, all_values)
    dscore = (prob_f * (dprob - delta) * scale_factor).astype(jnp.bfloat16)
    dquery = product('hgqk,khd->hgqd', dscore, all_keys)
    dkey = product('hgqk,hgqd->khd', dscore, q_heads)
    dvalue = product('hgqk,hgqd->khd', prob, g_heads)
    return (dquery, dkey, dvalue)

def rounded_term(term):
    narrow = lax.optimization_barrier(term.astype(jnp.bfloat16))
    return narrow.astype(jnp.float32)

def reference(queries, own_keys, own_values, prefix_keys, prefix_values, out_grad, lengths, advantage_sign):
    groups = QH // KVH
    scale_factor = 1.0 / math.sqrt(DH)
    total_tokens = jnp.sum(lengths).astype(jnp.float32)
    weight = (2 * advantage_sign - 1).astype(jnp.float32) * (RESPONSES * RLEN / total_tokens)
    prompt_keys = prefix_keys.reshape(PREFIX, KVH, DH)
    prompt_values = prefix_values.reshape(PREFIX, KVH, DH)
    position = jnp.arange(RLEN, dtype=jnp.int32)
    key_index = jnp.arange(PREFIX + RLEN, dtype=jnp.int32)
    visible = (key_index[None, :] < PREFIX) | (key_index[None, :] - PREFIX <= position[:, None])

    def one_response(carry, inputs):
        q_rows, k_rows, v_rows, g_rows, length, scale_weight = inputs
        all_keys = jnp.concatenate([prompt_keys, k_rows.reshape(RLEN, KVH, DH)], 0)
        all_values = jnp.concatenate([prompt_values, v_rows.reshape(RLEN, KVH, DH)], 0)
        live_mask = (position < length).astype(jnp.float32)
        grad_eff = (g_rows.astype(jnp.float32) * scale_weight * live_mask[:, None]).astype(jnp.bfloat16)
        q_heads = q_rows.reshape(RLEN, KVH, groups, DH).transpose(1, 2, 0, 3)
        g_heads = grad_eff.reshape(RLEN, KVH, groups, DH).transpose(1, 2, 0, 3)
        dquery, dkey, dvalue = attend(q_heads, g_heads, all_keys, all_values, visible, scale_factor)
        query_rows = dquery.transpose(2, 0, 1, 3).reshape(RLEN, QH * DH).astype(jnp.bfloat16)
        key_rows = dkey[PREFIX:].reshape(RLEN, KVH * DH).astype(jnp.bfloat16)
        value_rows = dvalue[PREFIX:].reshape(RLEN, KVH * DH).astype(jnp.bfloat16)
        carry = (carry[0] + rounded_term(dkey[:PREFIX]), carry[1] + rounded_term(dvalue[:PREFIX]))
        return (carry, (query_rows, key_rows, value_rows))
    start = (jnp.zeros((PREFIX, KVH, DH), jnp.float32), jnp.zeros((PREFIX, KVH, DH), jnp.float32))
    inputs = (queries.reshape(RESPONSES, RLEN, QH * DH), own_keys.reshape(RESPONSES, RLEN, KVH * DH), own_values.reshape(RESPONSES, RLEN, KVH * DH), out_grad.reshape(RESPONSES, RLEN, QH * DH), lengths, weight)
    sums, stacked = lax.scan(one_response, start, inputs)
    query_grad = stacked[0].reshape(RESPONSES * RLEN, QH * DH)
    own_key_grad = stacked[1].reshape(RESPONSES * RLEN, KVH * DH)
    own_value_grad = stacked[2].reshape(RESPONSES * RLEN, KVH * DH)
    prefix_key_grad = sums[0].reshape(PREFIX, KVH * DH).astype(jnp.bfloat16)
    prefix_value_grad = sums[1].reshape(PREFIX, KVH * DH).astype(jnp.bfloat16)
    return (query_grad, own_key_grad, own_value_grad, prefix_key_grad, prefix_value_grad)
```

```python
import functools
import math

import jax
import jax.numpy as jnp
from jax import lax
from jax.experimental import pallas as pl
from jax.experimental.pallas import tpu as pltpu
from jax.sharding import PartitionSpec as P

DH = 128
MESH = pl.DeviceIdType.MESH
F32 = jnp.float32
BF16 = jnp.bfloat16
SCALE = 1.0 / math.sqrt(DH)
LOG2 = SCALE * math.log2(math.e)
CHUNK = 128
SUP = 256
SUPS = 9
LEN_ROWS = 16
PACK = 2 * CHUNK + LEN_ROWS
RING = 8
A, B = 0, 1
UP, DOWN = 0, 1


def slot(stream, distance):
    if distance == 0:
        return stream
    if abs(distance) == 4:
        return 14 + stream
    return 2 + 4 * (abs(distance) - 1) + 2 * stream + (0 if distance > 0 else 1)


def dot(left, right):
    return jnp.dot(left, right, preferred_element_type=F32)


def kernel(
    heads, q_ref, ok_ref, ov_ref, pk_ref, pv_ref, g_ref, len_ref, sign_ref,
    qg_ref, okg_ref, ovg_ref, pkg_ref, pvg_ref,
    kv, q2, g2, qt, gt, kt, e_ref, d_ref, top, norm, delta, factor, home, send, send4, recv, recv4, x_send, x_recv,
    gather_send_sem, gather_recv_sem, reduce_send_sem, reduce_recv_sem,
):
    me = lax.axis_index("resp")
    ring = me % RING
    base = me - ring
    up = base + (ring + 1) % RING
    down = base + (ring + RING - 1) % RING
    partner = (me + RING) % (2 * RING)
    rows = q_ref.shape[0]

    barrier = pltpu.get_barrier_semaphore()
    for other in (up, down, partner):
        pl.semaphore_signal(barrier, inc=1, device_id={"resp": other}, device_id_type=MESH)

    length = len_ref[0]
    kv[0, 0:CHUNK, :] = pk_ref[...]
    kv[0, CHUNK : 2 * CHUNK, :] = pv_ref[...]
    kv[0, 2 * CHUNK :, :] = jnp.full((LEN_ROWS, DH), length, jnp.int32).astype(F32).astype(BF16)

    def remote(src, dst, sems, index, other):
        return pltpu.make_async_remote_copy(
            src_ref=src, dst_ref=dst, send_sem=sems[0].at[index], recv_sem=sems[1].at[index],
            device_id={"resp": other}, device_id_type=MESH,
        )

    gather_sems = (gather_send_sem, gather_recv_sem)
    reduce_sems = (reduce_send_sem, reduce_recv_sem)

    def gather_copy(stream, hop, way):
        sign, other = (-1, up) if way == UP else (1, down)
        index = 8 * stream + 2 * (hop - 1) + way
        src, dst = kv.at[slot(stream, sign * (hop - 1))], kv.at[slot(stream, sign * hop)]
        if hop == 4:
            part = pl.ds(0, CHUNK) if way == UP else pl.ds(CHUNK, PACK - CHUNK)
            src, dst = src.at[part], dst.at[part]
        return remote(src, dst, gather_sems, index, other)

    gathers = {
        (stream, hop, way): gather_copy(stream, hop, way)
        for stream in (A, B) for hop in (1, 2, 3, 4) for way in (UP, DOWN)
    }
    cross = remote(kv.at[0], kv.at[1], gather_sems, 16, partner)

    def gather_start(stream, hop):
        for way in (UP, DOWN):
            gathers[stream, hop, way].start()

    def gather_wait(stream, hop):
        for way in (UP, DOWN):
            gathers[stream, hop, way].wait_recv()

    pl.semaphore_wait(barrier, 3)
    gather_start(A, 1)
    cross.start()

    token = lax.broadcasted_iota(jnp.int32, (rows, DH), 0)
    for h in range(heads):
        columns = slice(h * DH, (h + 1) * DH)
        q_head = q_ref[:, columns]
        g_head = jnp.where(token < length, g_ref[:, columns].astype(F32), 0.0).astype(BF16)
        q2[h * rows : (h + 1) * rows, :] = q_head
        g2[h * rows : (h + 1) * rows, :] = g_head
        qt[h] = q_head.T
        gt[h] = g_head.T

    def keys_of(c):
        if c == 0:
            return ok_ref[...]
        first = 2 * (c - 1)
        return jnp.concatenate([kv[first, 0:CHUNK, :], kv[first + 1, 0:CHUNK, :]], 0)

    def values_of(c):
        if c == 0:
            return ov_ref[...]
        first = 2 * (c - 1)
        return jnp.concatenate([kv[first, CHUNK : 2 * CHUNK, :], kv[first + 1, CHUNK : 2 * CHUNK, :]], 0)

    def forward(c):
        span = slice(c * SUP, (c + 1) * SUP)
        kt[:, span] = keys_of(c).T

        def one_head(h):
            scores = dot(keys_of(c), qt[h])
            if c == 0:
                key_pos = lax.broadcasted_iota(jnp.int32, (SUP, rows), 0)
                token_pos = lax.broadcasted_iota(jnp.int32, (SUP, rows), 1)
                scores = jnp.where(key_pos <= token_pos, scores, -1e30)
            high = jnp.max(scores, axis=0, keepdims=True)
            expo = jnp.exp2((scores - high) * LOG2)
            dprob = dot(values_of(c), gt[h])
            top[c, pl.ds(h, 1), :] = high
            norm[c, pl.ds(h, 1), :] = jnp.sum(expo, axis=0, keepdims=True)
            delta[c, pl.ds(h, 1), :] = jnp.sum(expo * dprob, axis=0, keepdims=True)
            e_ref[h, span, :] = expo.astype(BF16)
            d_ref[h, span, :] = dprob.astype(BF16)

        def pair(i, _):
            one_head(2 * i)
            one_head(2 * i + 1)
            return 0

        lax.fori_loop(0, heads // 2, pair, 0)

    forward(0)
    gather_wait(A, 1)
    gather_start(A, 2)
    forward(2)
    cross.wait_recv()
    gather_start(B, 1)
    forward(1)
    gather_wait(A, 2)
    gather_start(A, 3)
    forward(4)
    gather_wait(B, 1)
    gather_start(B, 2)
    forward(3)
    gather_wait(A, 3)
    gather_start(A, 4)
    forward(6)
    gather_wait(B, 2)
    gather_start(B, 3)
    forward(5)
    gather_wait(B, 3)
    gather_start(B, 4)
    forward(7)
    gather_wait(A, 4)
    gather_wait(B, 4)
    forward(8)

    live = kv[0, 2 * CHUNK :, :].astype(F32)
    for s in range(1, 16):
        live = live + kv[s, 2 * CHUNK :, :].astype(F32)
    sign_value = (2 * sign_ref[0] - 1).astype(F32)
    weight = (sign_value * (2 * RING * rows)) / live[0:heads, :]
    weight = jnp.concatenate([weight] * (rows // DH), 1)

    high = top[0]
    for c in range(1, SUPS):
        high = jnp.maximum(high, top[c])
    shares = [jnp.exp2((top[c] - high) * LOG2) for c in range(SUPS)]
    total, mean = shares[0] * norm[0], shares[0] * delta[0]
    for c in range(1, SUPS):
        total = total + shares[c] * norm[c]
        mean = mean + shares[c] * delta[c]
    inverse = 1.0 / total
    mean = mean * inverse
    inverse = inverse * weight
    for c in range(SUPS):
        factor[c] = shares[c] * inverse
    delta[0] = mean

    def spread(row):
        return jnp.broadcast_to(row, (16, rows)).astype(BF16)[None]

    def tile(block):
        return block.reshape(SUP // 16, 16, rows)

    def backward(c):
        span = slice(c * SUP, (c + 1) * SUP)
        probs, dscores = [], []
        for h in range(heads):
            prob = tile(e_ref[h, span, :]) * spread(factor[c, h : h + 1, :])
            dscore = (prob * (tile(d_ref[h, span, :]) - spread(delta[0, h : h + 1, :]))).reshape(SUP, rows)
            d_ref[h, span, :] = dscore
            probs.append(prob.reshape(SUP, rows))
            dscores.append(dscore)
        value_grad = dot(jnp.concatenate(probs, 1), g2[...])
        key_grad = dot(jnp.concatenate(dscores, 1), q2[...]) * SCALE
        return key_grad, value_grad

    def reduce_copy(stream, step, way):
        other = up if way == UP else down
        index = 8 * stream + 2 * (step - 1) + way
        if step == 4:
            return remote(send4.at[stream, way], recv4.at[stream, way], reduce_sems, index, other)
        return remote(send.at[stream, way, step - 1], recv.at[stream, way, step - 1], reduce_sems, index, other)

    reduces = {
        (stream, step, way): reduce_copy(stream, step, way)
        for stream in (A, B) for step in (1, 2, 3, 4) for way in (UP, DOWN)
    }
    back = remote(x_send, x_recv, reduce_sems, 16, partner)

    key_grad, value_grad = backward(8)
    for stream in (B, A):
        part = slice(stream * CHUNK, (stream + 1) * CHUNK)
        send4[stream, UP] = key_grad[part].astype(BF16)
        send4[stream, DOWN] = value_grad[part].astype(BF16)
        for way in (UP, DOWN):
            reduces[stream, 4, way].start()

    for step in (3, 2, 1):
        for stream in (B, A):
            key_grad, value_grad = backward(2 * step + stream)
            for way in (UP, DOWN):
                part = slice(way * CHUNK, (way + 1) * CHUNK)
                key_part, value_part = key_grad[part], value_grad[part]
                reduces[stream, step + 1, way].wait_recv()
                if step == 3:
                    if way == UP:
                        key_part = key_part + recv4[stream, way].astype(F32)
                    else:
                        value_part = value_part + recv4[stream, way].astype(F32)
                else:
                    key_part = key_part + recv[stream, way, step, 0:CHUNK, :].astype(F32)
                    value_part = value_part + recv[stream, way, step, CHUNK:, :].astype(F32)
                send[stream, way, step - 1, 0:CHUNK, :] = key_part.astype(BF16)
                send[stream, way, step - 1, CHUNK:, :] = value_part.astype(BF16)
                reduces[stream, step, way].start()

    key_grad, value_grad = backward(1)
    for stream in (A, B):
        part = slice(stream * CHUNK, (stream + 1) * CHUNK)
        home[stream, 0:CHUNK, :] = key_grad[part]
        home[stream, CHUNK:, :] = value_grad[part]
    key_grad, value_grad = backward(0)
    okg_ref[...] = key_grad.astype(BF16)
    ovg_ref[...] = value_grad.astype(BF16)

    def query_head(h, _):
        grad = dot(kt[...], d_ref[h]) * SCALE
        qg_ref[:, pl.ds(pl.multiple_of(h * DH, DH), DH)] = grad.T.astype(BF16)
        return 0

    def collect(stream):
        result = home[stream]
        for way in (UP, DOWN):
            reduces[stream, 1, way].wait_recv()
            result = result + recv[stream, way, 0].astype(F32)
        return result

    lax.fori_loop(0, heads // 2, query_head, 0)
    x_send[...] = collect(B).astype(BF16)
    back.start()
    lax.fori_loop(heads // 2, heads, query_head, 0)
    mine = collect(A)
    back.wait_recv()
    mine = mine + x_recv[...].astype(F32)
    pkg_ref[...] = mine[0:CHUNK].astype(BF16)
    pvg_ref[...] = mine[CHUNK:].astype(BF16)

    for copy in [*gathers.values(), cross, *reduces.values(), back]:
        copy.wait_send()


def shards(queries, own_keys, own_values, prefix_keys, prefix_values, out_grad, lengths, advantage_sign):
    rows = queries.shape[0]
    heads = queries.shape[1] // DH
    vmem = pl.BlockSpec(memory_space=pltpu.VMEM)
    smem = pl.BlockSpec(memory_space=pltpu.SMEM)
    like = lambda x: jax.ShapeDtypeStruct(x.shape, BF16)
    keys = SUP * SUPS
    return pl.pallas_call(
        functools.partial(kernel, heads),
        out_shape=(like(queries), like(own_keys), like(own_values), like(prefix_keys), like(prefix_values)),
        in_specs=[vmem] * 6 + [smem] * 2,
        out_specs=(vmem,) * 5,
        scratch_shapes=[
            pltpu.VMEM((2 * RING, PACK, DH), BF16),
            pltpu.VMEM((heads * rows, DH), BF16),
            pltpu.VMEM((heads * rows, DH), BF16),
            pltpu.VMEM((heads, DH, rows), BF16),
            pltpu.VMEM((heads, DH, rows), BF16),
            pltpu.VMEM((DH, keys), BF16),
            pltpu.VMEM((heads, keys, rows), BF16),
            pltpu.VMEM((heads, keys, rows), BF16),
            pltpu.VMEM((SUPS, heads, rows), F32),
            pltpu.VMEM((SUPS, heads, rows), F32),
            pltpu.VMEM((SUPS, heads, rows), F32),
            pltpu.VMEM((SUPS, heads, rows), F32),
            pltpu.VMEM((2, 2 * CHUNK, DH), F32),
            pltpu.VMEM((2, 2, 3, 2 * CHUNK, DH), BF16),
            pltpu.VMEM((2, 2, CHUNK, DH), BF16),
            pltpu.VMEM((2, 2, 3, 2 * CHUNK, DH), BF16),
            pltpu.VMEM((2, 2, CHUNK, DH), BF16),
            pltpu.VMEM((2 * CHUNK, DH), BF16),
            pltpu.VMEM((2 * CHUNK, DH), BF16),
            pltpu.SemaphoreType.DMA((17,)),
            pltpu.SemaphoreType.DMA((17,)),
            pltpu.SemaphoreType.DMA((17,)),
            pltpu.SemaphoreType.DMA((17,)),
        ],
        compiler_params=pltpu.CompilerParams(
            collective_id=0, has_side_effects=True, vmem_limit_bytes=48 * 1024 * 1024
        ),
        cost_estimate=pl.CostEstimate(
            flops=10 * heads * rows * keys * DH, bytes_accessed=4 * heads * rows * DH * 2, transcendentals=heads * rows * keys
        ),
    )(queries, own_keys, own_values, prefix_keys, prefix_values, out_grad, lengths, advantage_sign)


def solution(mesh):
    split = P(("grp", "resp"), "tp")
    flat = P(("grp", "resp"))
    return jax.shard_map(
        shards, mesh=mesh, in_specs=(split,) * 6 + (flat,) * 2, out_specs=(split,) * 5, check_vma=False
    )
```
